32 devices in a mesh: rep: 1, dev: 32 (over z, y, x, core).
Axes of the slice: x: 2, y: 2, z: 4, core: 2. Of those that a mesh axis runs over, the one named last changes fastest.
Arguments:
- tokens: bfloat16 [4096, 7168], P(('rep', 'dev')), may hold values from -6 to 6
- routes: int32 [4096, 2], P(('rep', 'dev')), may hold values from 0 to 3, all different within a row; in each aligned block of 128 rows (0 to 127, 128 to 255, ...) at most 72 rows name the same one
- route_weight: bfloat16 [4096, 2], P(('rep', 'dev')), may hold values from 0.099609375 to 1
- gate_values: bfloat16 [28672, 1024], P('dev'), may hold values from -0.0625 to 0.0625
- gate_scales: float32 [224, 8], P('dev'), may hold values from 0.5 to 2
- up_values: bfloat16 [28672, 1024], P('dev'), may hold values from -0.0625 to 0.0625
- up_scales: float32 [224, 8], P('dev'), may hold values from 0.5 to 2
- down_values: bfloat16 [1024, 28672], P(None, 'dev'), may hold values from -0.1875 to 0.1875
- down_scales: float32 [8, 224], P(None, 'dev'), may hold values from 0.5 to 2
Outputs:
- mixed: bfloat16 [4096, 7168], P(('rep', 'dev'))
The draws below stay inside these ranges and needn't reach their ends.
Inputs may be any that keep to these rules, and one draw needn't show every extreme that they name: `routes`: each token names 2 different experts. Among the tokens of one device (aligned blocks of 128 rows) no expert is named by more than 72 tokens, a bound that some block reaches.
All inputs are finite; a program needn't handle non-finite values.
Results may differ from the reference program's by a relative error of at most 0.0078.
Values may be sent and summed in bfloat16 or wider, within the bound.
A program may use at most 128 MiB of HBM per device.

```python
import math
import jax
import jax.numpy as jnp
import numpy as np
from jax import lax

D = 7168
FF = 1024
BLOCK = 128
TOPK = 2
TOK_DEV = 128
EXPERTS = 4
CAP = 72
TOKENS = 4096
N_DEV = 32


def level_of(rng, shape, cuts, low, high):
    level = 1.0
    for dim, parts in cuts:
        heights = jax.random.uniform(jax.random.fold_in(jax.random.fold_in(rng, 6), dim), (parts,), jnp.float32, low / len(cuts), high / len(cuts))
        level = level * jnp.repeat(jnp.exp(heights), shape[dim] // parts).reshape((-1,) + (1,) * (len(shape) - 1 - dim))
    return level


def deal_out(rng, own, number, rows, amount, top, most, skew):
    order = jax.random.permutation(rng, amount)
    crowded, common = portions_of(amount, rows * top, most, skew, True), portions_of(amount, rows * top, most, skew, False)
    places = jnp.arange(amount)

    def named(tallies, rotation):
        used = int((tallies > 0).sum())
        fixed = max(1, used // 4)
        passed = fixed + (places - fixed + rotation * (used - fixed)) % max(1, amount - fixed)
        return jnp.zeros((amount,), jnp.int32).at[order[jnp.where(places < fixed, places, passed)]].set(jnp.asarray(tallies, jnp.int32))

    tallies = jnp.where(number % 4 == 0, named(crowded, number // 4), named(common, number - number // 4 - 1))
    mixed = jax.random.permutation(jax.random.fold_in(own, 3), amount)
    source_of, receiver = mixed[0:amount // 2 * 2:2], mixed[1:amount // 2 * 2:2]
    margin = jnp.minimum(tallies[source_of] - 1, most - tallies[receiver]) // 2
    margin = jnp.where((source_of == order[0]) | (receiver == order[0]) | (tallies[receiver] == 0), 0, jnp.maximum(margin, 0))
    passed = jax.random.randint(jax.random.fold_in(own, 4), (amount // 2,), 0, 1 << 20) % (margin + 1)
    tallies = tallies.at[source_of].add(-passed).at[receiver].add(passed)
    items = jnp.searchsorted(jnp.cumsum(tallies), jnp.arange(rows * top), side="right").astype(jnp.int32)
    table = items.reshape(top, rows).T
    table = table[jax.random.permutation(jax.random.fold_in(own, 1), rows)]
    rotation = jax.random.randint(jax.random.fold_in(own, 2), (rows, 1), 0, top)
    return jnp.take_along_axis(table, (jnp.arange(top)[None, :] + rotation) % top, axis=1)


def portions_of(count, total, most, slope, full):
    portions = [(1 << 20) // math.isqrt(standing ** slope) + 1 for standing in range(1, count + 1)]
    largest = most if full else min(most, max(-(-total // count), total * portions[0] // sum(portions)))
    least = 1 if total - largest >= count - 1 else 0
    holding, rest = [largest] + [least] * (count - 1), total - largest - least * (count - 1)
    while rest > 0:
        movable = [i for i in range(1, count) if holding[i] < largest] or [i for i in range(1, count) if holding[i] < most]
        whole, budget = sum([portions[i] for i in movable]), rest
        for i in movable:
            extra = min(most - holding[i], max(1, budget * portions[i] // whole), rest)
            holding[i] = holding[i] + extra
            rest = rest - extra
    return np.array(holding)


def bell_draw(own_key, dims, spread, reach, split=(), held_as=jnp.bfloat16):
    array = spread * jax.random.normal(own_key, dims, jnp.float32)
    if split:
        array = array * level_of(own_key, dims, split, -0.22, 0.18)
    return jnp.clip(array, -reach, reach).astype(held_as)


def setup_inputs(seed: int = 0, part: int = 0) -> dict:
    splits = jax.random.split(jax.random.key(seed), 10)
    part_keys = jax.random.split(jax.random.fold_in(splits[9], part), 10)
    tokens = bell_draw(part_keys[0], (TOKENS, D), 1.0, 6.0, ((0, 32),))
    routes_keys = jax.random.split(jax.random.fold_in(part_keys[1], 1), TOKENS // TOK_DEV)
    routes_turns = jax.random.permutation(jax.random.fold_in(part_keys[1], 3), TOKENS // TOK_DEV)
    routes = jax.vmap(lambda own, number: deal_out(jax.random.fold_in(part_keys[1], 2), own, number, TOK_DEV, EXPERTS, TOPK, CAP, 1))(routes_keys, routes_turns).reshape((TOKENS, TOPK))
    route_weight = jnp.clip(0.099609375 + 0.9003906 * jax.random.uniform(part_keys[2], (TOKENS, TOPK), jnp.float32) ** level_of(part_keys[2], (TOKENS, TOPK), ((0, 32),), -0.2, 0.2), 0.099609375, 1.0).astype(jnp.bfloat16)
    gate_values = bell_draw(splits[3], (EXPERTS * D, FF), D ** -0.5, 0.0625, ((0, 32),))
    gate_scales = jnp.clip(jnp.exp(math.log(2.0) - 1.3862944 * jax.random.uniform(splits[4], (EXPERTS * D // BLOCK, FF // BLOCK), jnp.float32) ** level_of(splits[4], (EXPERTS * D // BLOCK, FF // BLOCK), ((0, 32),), -0.2, 0.2)), 0.5, 2.0)
    up_values = bell_draw(splits[5], (EXPERTS * D, FF), D ** -0.5, 0.0625, ((0, 32),))
    up_scales = jnp.clip(jnp.exp(math.log(2.0) - 1.3862944 * jax.random.uniform(splits[6], (EXPERTS * D // BLOCK, FF // BLOCK), jnp.float32) ** level_of(splits[6], (EXPERTS * D // BLOCK, FF // BLOCK), ((0, 32),), -0.2, 0.2)), 0.5, 2.0)
    down_values = bell_draw(splits[7], (FF, EXPERTS * D), FF ** -0.5, 0.1875, ((1, 32),))
    down_scales = jnp.clip(jnp.exp(math.log(2.0) - 1.3862944 * jax.random.uniform(splits[8], (FF // BLOCK, EXPERTS * D // BLOCK), jnp.float32) ** level_of(splits[8], (FF // BLOCK, EXPERTS * D // BLOCK), ((1, 32),), -0.2, 0.2)), 0.5, 2.0)
    return {"tokens": tokens, "routes": routes, "route_weight": route_weight, "gate_values": gate_values, "gate_scales": gate_scales, "up_values": up_values, "up_scales": up_scales, "down_values": down_values, "down_scales": down_scales}


def dequantize(values, scales):
    rows_count, cols_count = values.shape
    grid = values.astype(jnp.float32).reshape(rows_count // BLOCK, BLOCK, cols_count // BLOCK, BLOCK)
    return (grid * scales[:, None, :, None]).reshape(rows_count, cols_count).astype(jnp.bfloat16)


def reference(tokens, routes, route_weight, gate_values, gate_scales, up_values, up_scales, down_values, down_scales):
    pairs = TOK_DEV * TOPK
    flat_routes = routes.reshape(N_DEV, pairs)
    one_hot = (flat_routes[..., None] == jnp.arange(EXPERTS, dtype=jnp.int32)).astype(jnp.int32)
    position = jnp.sum((jnp.cumsum(one_hot, axis=1) - 1) * one_hot, axis=-1)
    slot_ids = flat_routes * CAP + position
    sources = jnp.arange(N_DEV, dtype=jnp.int32)[:, None]
    token_ids = sources * TOK_DEV + (jnp.arange(pairs, dtype=jnp.int32) // TOPK)[None, :]
    table = jnp.full((N_DEV, EXPERTS * CAP), -1, jnp.int32).at[sources, slot_ids].set(token_ids)
    table = table.reshape(N_DEV, EXPERTS, CAP).transpose(1, 0, 2).reshape(EXPERTS, N_DEV * CAP)

    def expert_apply(operands):
        slot_tokens, gate_v, gate_s, up_v, up_s, down_v, down_s = operands
        safe_ids = jnp.maximum(slot_tokens, 0)
        inputs = jnp.where((slot_tokens >= 0)[:, None], tokens[safe_ids], jnp.zeros((), jnp.bfloat16))
        gate_part = jnp.dot(inputs, dequantize(gate_v, gate_s), preferred_element_type=jnp.float32)
        up_part = jnp.dot(inputs, dequantize(up_v, up_s), preferred_element_type=jnp.float32)
        hidden = (jax.nn.silu(gate_part) * up_part).astype(jnp.bfloat16)
        return jnp.dot(hidden, dequantize(down_v, down_s), preferred_element_type=jnp.float32).astype(jnp.bfloat16)

    outputs = lax.map(expert_apply, (
        table,
        gate_values.reshape(EXPERTS, D, FF),
        gate_scales.reshape(EXPERTS, D // BLOCK, FF // BLOCK),
        up_values.reshape(EXPERTS, D, FF),
        up_scales.reshape(EXPERTS, D // BLOCK, FF // BLOCK),
        down_values.reshape(FF, EXPERTS, D).transpose(1, 0, 2),
        down_scales.reshape(FF // BLOCK, EXPERTS, D // BLOCK).transpose(1, 0, 2)))
    global_rows = flat_routes * (N_DEV * CAP) + sources * CAP + position
    picked = outputs.reshape(EXPERTS * N_DEV * CAP, D)[global_rows.reshape(-1)]
    picked = picked.reshape(TOKENS, TOPK, D).astype(jnp.float32)
    weights = route_weight.astype(jnp.float32)[:, :, None]
    return jnp.sum(picked * weights, axis=1).astype(jnp.bfloat16)
```

```python
import functools

import jax
import jax.numpy as jnp
from jax import lax
from jax.experimental import pallas as pl
from jax.experimental.pallas import tpu as pltpu
from jax.sharding import PartitionSpec as P

BLOCK = 128
GROUP = 8
CHIPS = GROUP // 2
MESH = pl.DeviceIdType.MESH


def slot_tables(routes, route_weight, experts, padded, capacity):
    tok_count, top_count = routes.shape
    flat_routes = routes.reshape(-1)
    one_hot = (flat_routes[:, None] == jnp.arange(experts, dtype=jnp.int32)[None, :]).astype(
        jnp.int32
    )
    position = jnp.sum((jnp.cumsum(one_hot, axis=0) - 1) * one_hot, axis=1)
    slot_ids = (flat_routes * padded + position).reshape(tok_count, top_count)
    slot_range = jnp.arange(experts * padded, dtype=jnp.int32)
    placing = jnp.zeros((experts * padded, tok_count), jnp.float32)
    weighting = jnp.zeros((tok_count, experts * padded), jnp.float32)
    for choose in range(top_count):
        match = slot_ids[:, choose][None, :] == slot_range[:, None]
        placing = placing + match.astype(jnp.float32)
        match = slot_ids[:, choose][:, None] == slot_range[None, :]
        weighting = weighting + jnp.where(
            match, route_weight[:, choose].astype(jnp.float32)[:, None], 0.0
        )
    placing = placing.astype(jnp.bfloat16).reshape(experts, padded, tok_count)
    weighting = weighting.astype(jnp.bfloat16).reshape(tok_count, experts, padded)
    none_p, none_w = jnp.zeros_like(placing), jnp.zeros_like(weighting)
    place = jnp.concatenate(
        [
            jnp.concatenate([placing, none_p], axis=2),
            jnp.concatenate([none_p, placing], axis=2),
        ],
        axis=1,
    )
    weigh = jnp.stack(
        [
            jnp.concatenate([weighting, none_w], axis=2).reshape(tok_count, -1),
            jnp.concatenate([none_w, weighting], axis=2).reshape(tok_count, -1),
        ]
    )
    return place, weigh


def kernel(
    experts,
    padded,
    tokens,
    place,
    weigh,
    gate_values,
    gate_scales,
    up_values,
    up_scales,
    down_values,
    down_scales,
    out,
    raw_gate,
    raw_up,
    raw_down,
    both,
    down,
    sent,
    got,
    own,
    part_out,
    part_in,
    hidden,
    back_out,
    back_in,
    raw_sem,
    wide_sem,
    sent_sem,
    got_sem,
    part_out_sem,
    part_in_sem,
    hid_out_sem,
    hid_in_sem,
    back_out_sem,
    back_in_sem,
):
    me = lax.axis_index("dev")
    expert = me // GROUP
    chip = (me % GROUP) // 2
    core = me % 2
    width = gate_values.shape[0]
    cols = part_in.shape[-1]
    half = cols // 2

    def device(group, place_in):
        return group * GROUP + place_in * 2 + core

    def remote(src, dst, send_sem, recv_sem, target):
        return pltpu.make_async_remote_copy(
            src_ref=src,
            dst_ref=dst,
            send_sem=send_sem,
            recv_sem=recv_sem,
            device_id={"dev": target},
            device_id_type=MESH,
        )

    raw = [
        pltpu.make_async_copy(gate_values, raw_gate, raw_sem.at[0]),
        pltpu.make_async_copy(up_values, raw_up, raw_sem.at[1]),
        pltpu.make_async_copy(down_values, raw_down, raw_sem.at[2]),
    ]
    for copy in raw:
        copy.start()

    barrier = pltpu.get_barrier_semaphore()
    partner = expert * GROUP + chip * 2 + (1 - core)
    pl.semaphore_signal(barrier, inc=1, device_id={"dev": partner}, device_id_type=MESH)

    @pl.loop(1, experts * CHIPS)
    def _(step):
        other = lax.rem(expert * CHIPS + chip + step, experts * CHIPS)
        pl.semaphore_signal(
            barrier, inc=1, device_id={"dev": other * 2 + core}, device_id_type=MESH
        )

    pl.semaphore_wait(barrier, experts * CHIPS)

    def dispatch(step, q):
        group = expert ^ step
        return remote(
            sent.at[step, q],
            got.at[expert, chip],
            sent_sem.at[step, q],
            got_sem.at[expert, chip],
            device(group, q),
        )

    def is_self(step, q):
        return jnp.logical_and(step == 0, q == chip)

    @pl.loop(0, experts)
    def _(turn):
        step = experts - 1 - turn
        for q in range(CHIPS):
            low = tokens[:, 2 * q * width : (2 * q + 1) * width]
            high = tokens[:, (2 * q + 1) * width : (2 * q + 2) * width]
            rows = jnp.dot(
                place[expert ^ step],
                jnp.concatenate([low, high], axis=0),
                preferred_element_type=jnp.float32,
            ).astype(jnp.bfloat16)

            @pl.when(is_self(step, q))
            def _():
                got[expert, chip] = rows

            @pl.when(jnp.logical_not(is_self(step, q)))
            def _():
                sent[step, q] = rows
                dispatch(step, q).start()

    for copy in raw:
        copy.wait()

    @pl.loop(0, width // BLOCK)
    def _(r):
        span = pl.ds(pl.multiple_of(r * BLOCK, BLOCK), BLOCK)
        gate = (raw_gate[span, :].astype(jnp.float32) * gate_scales[pl.ds(r, 1), :]).astype(
            jnp.bfloat16
        )
        up = (raw_up[span, :].astype(jnp.float32) * up_scales[pl.ds(r, 1), :]).astype(jnp.bfloat16)
        for q in range(CHIPS):
            both[core, q, span, 0:half] = gate[:, q * half : (q + 1) * half]
            both[core, q, span, half:cols] = up[:, q * half : (q + 1) * half]

    wide = [
        remote(both.at[core], both.at[core], wide_sem.at[0], wide_sem.at[1], partner),
        remote(down.at[core], down.at[core], wide_sem.at[2], wide_sem.at[3], partner),
    ]
    wide[0].start()

    @pl.loop(0, raw_down.shape[0] // BLOCK)
    def _(r):
        span = pl.ds(pl.multiple_of(r * BLOCK, BLOCK), BLOCK)
        down[core, span, :] = (
            raw_down[span, :].astype(jnp.float32) * down_scales[pl.ds(r, 1), :]
        ).astype(jnp.bfloat16)

    wide[1].start()
    for copy in wide:
        copy.wait_recv()

    def part_copy(step, d):
        return remote(
            part_out.at[step, d - 1],
            part_in.at[step, d - 1],
            part_out_sem.at[step, d - 1],
            part_in_sem.at[step, d - 1],
            device(expert, chip ^ d),
        )

    def hidden_copy(step, d):
        return remote(
            hidden.at[step, chip],
            hidden.at[step, chip],
            hid_out_sem.at[step, d - 1],
            hid_in_sem.at[step, d - 1],
            device(expert, chip ^ d),
        )

    def back_copy(step, q):
        return remote(
            back_out.at[step, q],
            back_in.at[chip, expert],
            back_out_sem.at[step, q],
            back_in_sem.at[chip, expert],
            device(expert ^ step, q),
        )

    def widen(step):
        source = expert ^ step
        for q in range(CHIPS):

            @pl.when(jnp.logical_not(is_self(step, q)))
            def _():
                remote(
                    sent.at[step, q],
                    got.at[source, q],
                    sent_sem.at[step, q],
                    got_sem.at[source, q],
                    device(source, q),
                ).wait_recv()

        rows = got[source].astype(jnp.float32)
        low = rows[:, :padded].reshape(CHIPS * padded, width).astype(jnp.bfloat16)
        high = rows[:, padded:].reshape(CHIPS * padded, width).astype(jnp.bfloat16)
        for d in (3, 1, 2, 0):
            total = jnp.dot(low, both[0, chip ^ d], preferred_element_type=jnp.float32)
            total = total + jnp.dot(high, both[1, chip ^ d], preferred_element_type=jnp.float32)
            if d == 0:
                own[step] = total
            else:
                part_out[step, d - 1] = total.astype(jnp.bfloat16)
                part_copy(step, d).start()

    def activate(step):
        total = own[step]
        for d in (1, 2, 3):
            part_copy(step, d).wait_recv()
            total = total + part_in[step, d - 1].astype(jnp.float32)
        gate, up = total[:, :half], total[:, half:]
        hidden[step, chip] = (gate / (1.0 + jnp.exp(-gate)) * up).astype(jnp.bfloat16)
        for d in (3, 1, 2):
            hidden_copy(step, d).start()

    def narrow(step):
        for d in (1, 2, 3):
            remote(
                hidden.at[step, chip],
                hidden.at[step, chip ^ d],
                hid_out_sem.at[step, d - 1],
                hid_in_sem.at[step, d - 1],
                device(expert, chip ^ d),
            ).wait_recv()
        whole = jnp.concatenate([hidden[step, q] for q in range(CHIPS)], axis=1)
        low = jnp.dot(whole, down[0], preferred_element_type=jnp.float32)
        high = jnp.dot(whole, down[1], preferred_element_type=jnp.float32)
        for q in range(CHIPS):
            span = slice(q * padded, (q + 1) * padded)
            rows = jnp.concatenate([low[span], high[span]], axis=0).astype(jnp.bfloat16)

            @pl.when(is_self(step, q))
            def _():
                back_in[chip, expert] = rows

            @pl.when(jnp.logical_not(is_self(step, q)))
            def _():
                back_out[step, q] = rows
                back_copy(step, q).start()

    @pl.loop(0, experts + 1)
    def _(turn):
        @pl.when(turn < experts)
        def _():
            widen(turn)

        @pl.when(turn > 0)
        def _():
            activate(turn - 1)
            narrow(turn - 1)

    for q in range(CHIPS):

        @pl.loop(0, experts)
        def _(step):
            @pl.when(jnp.logical_not(is_self(step, q)))
            def _():
                remote(
                    back_out.at[step, q],
                    back_in.at[q, expert ^ step],
                    back_out_sem.at[step, q],
                    back_in_sem.at[q, expert ^ step],
                    device(expert ^ step, q),
                ).wait_recv()

        rows = back_in[q].reshape(experts * 2 * padded, width)
        for h in range(2):
            start = (2 * q + h) * width
            out[:, start : start + width] = jnp.dot(
                weigh[h], rows, preferred_element_type=jnp.float32
            ).astype(jnp.bfloat16)

    for copy in wide:
        copy.wait_send()

    @pl.loop(0, experts)
    def _(step):
        for d in (1, 2, 3):
            part_copy(step, d).wait_send()
            hidden_copy(step, d).wait_send()
        for q in range(CHIPS):

            @pl.when(jnp.logical_not(is_self(step, q)))
            def _():
                dispatch(step, q).wait_send()
                back_copy(step, q).wait_send()


def shards(
    tokens,
    routes,
    route_weight,
    gate_values,
    gate_scales,
    up_values,
    up_scales,
    down_values,
    down_scales,
):
    devices = lax.axis_size("dev")
    experts = devices // GROUP
    tok_count, model = tokens.shape
    top_count = routes.shape[1]
    capacity = min(tok_count, tok_count * top_count * 9 // (8 * experts))
    padded = -(-capacity // 8) * 8
    width, units = gate_values.shape
    cols = 2 * units // CHIPS
    place, weigh = slot_tables(routes, route_weight, experts, padded, capacity)
    spread = functools.partial(jnp.repeat, repeats=BLOCK, axis=1)
    vmem = pl.BlockSpec(memory_space=pltpu.VMEM)
    anywhere = pl.BlockSpec(memory_space=pl.ANY)
    bf16 = jnp.bfloat16
    rows = CHIPS * padded
    dma = pltpu.SemaphoreType.DMA
    return pl.pallas_call(
        functools.partial(kernel, experts, padded),
        out_shape=jax.ShapeDtypeStruct((tok_count, model), bf16),
        in_specs=[vmem, vmem, vmem, anywhere, vmem, anywhere, vmem, anywhere, vmem],
        out_specs=vmem,
        scratch_shapes=[
            pltpu.VMEM((width, units), bf16),
            pltpu.VMEM((width, units), bf16),
            pltpu.VMEM((units, width), bf16),
            pltpu.VMEM((2, CHIPS, width, cols), bf16),
            pltpu.VMEM((2, units, width), bf16),
            pltpu.VMEM((experts, CHIPS, 2 * padded, width), bf16),
            pltpu.VMEM((experts, CHIPS, 2 * padded, width), bf16),
            pltpu.VMEM((experts, rows, cols), jnp.float32),
            pltpu.VMEM((experts, CHIPS - 1, rows, cols), bf16),
            pltpu.VMEM((experts, CHIPS - 1, rows, cols), bf16),
            pltpu.VMEM((experts, CHIPS, rows, cols // 2), bf16),
            pltpu.VMEM((experts, CHIPS, 2 * padded, width), bf16),
            pltpu.VMEM((CHIPS, experts, 2 * padded, width), bf16),
            dma((3,)),
            dma((4,)),
            dma((experts, CHIPS)),
            dma((experts, CHIPS)),
            dma((experts, CHIPS - 1)),
            dma((experts, CHIPS - 1)),
            dma((experts, CHIPS - 1)),
            dma((experts, CHIPS - 1)),
            dma((experts, CHIPS)),
            dma((CHIPS, experts)),
        ],
        compiler_params=pltpu.CompilerParams(
            collective_id=0, has_side_effects=True, vmem_limit_bytes=60 * 1024 * 1024
        ),
    )(
        tokens,
        place,
        weigh,
        gate_values,
        spread(gate_scales),
        up_values,
        spread(up_scales),
        down_values,
        spread(down_scales),
    )


def solution(mesh):
    return jax.shard_map(
        shards,
        mesh=mesh,
        in_specs=(
            P(("rep", "dev"), None),
            P(("rep", "dev"), None),
            P(("rep", "dev"), None),
            P("dev", None),
            P("dev", None),
            P("dev", None),
            P("dev", None),
            P(None, "dev"),
            P(None, "dev"),
        ),
        out_specs=P(("rep", "dev"), None),
        check_vma=False,
    )
```

```python
import functools

import jax
import jax.numpy as jnp
from jax import lax
from jax.experimental import pallas as pl
from jax.experimental.pallas import tpu as pltpu
from jax.sharding import PartitionSpec as P

BLOCK = 128
GROUP = 8
CHIPS = GROUP // 2
MESH = pl.DeviceIdType.MESH


def slot_tables(routes, route_weight, experts, padded, capacity):
    tok_count, top_count = routes.shape
    flat_routes = routes.reshape(-1)
    one_hot = (flat_routes[:, None] == jnp.arange(experts, dtype=jnp.int32)[None, :]).astype(
        jnp.int32
    )
    position = jnp.sum((jnp.cumsum(one_hot, axis=0) - 1) * one_hot, axis=1)
    slot_ids = (flat_routes * padded + position).reshape(tok_count, top_count)
    slot_range = jnp.arange(experts * padded, dtype=jnp.int32)
    placing = jnp.zeros((experts * padded, tok_count), jnp.float32)
    weighting = jnp.zeros((tok_count, experts * padded), jnp.float32)
    for choose in range(top_count):
        match = slot_ids[:, choose][None, :] == slot_range[:, None]
        placing = placing + match.astype(jnp.float32)
        match = slot_ids[:, choose][:, None] == slot_range[None, :]
        weighting = weighting + jnp.where(
            match, route_weight[:, choose].astype(jnp.float32)[:, None], 0.0
        )
    placing = placing.astype(jnp.bfloat16).reshape(experts, padded, tok_count)
    weighting = weighting.astype(jnp.bfloat16).reshape(tok_count, experts, padded)
    none_p, none_w = jnp.zeros_like(placing), jnp.zeros_like(weighting)
    place = jnp.concatenate(
        [
            jnp.concatenate([placing, none_p], axis=2),
            jnp.concatenate([none_p, placing], axis=2),
        ],
        axis=1,
    )
    weigh = jnp.stack(
        [
            jnp.concatenate([weighting, none_w], axis=2).reshape(tok_count, -1),
            jnp.concatenate([none_w, weighting], axis=2).reshape(tok_count, -1),
        ]
    )
    return place, weigh


def kernel(
    experts,
    padded,
    tokens,
    place,
    weigh,
    gate_values,
    gate_scales,
    up_values,
    up_scales,
    down_values,
    down_scales,
    out,
    raw_gate,
    raw_up,
    raw_down,
    both,
    down,
    sent,
    got,
    own,
    part_out,
    part_in,
    hidden,
    back_out,
    back_in,
    raw_sem,
    wide_sem,
    sent_sem,
    got_sem,
    part_out_sem,
    part_in_sem,
    hid_out_sem,
    hid_in_sem,
    back_out_sem,
    back_in_sem,
):
    me = lax.axis_index("dev")
    expert = me // GROUP
    chip = (me % GROUP) // 2
    core = me % 2
    width = gate_values.shape[0]
    cols = part_in.shape[-1]
    half = cols // 2

    def device(group, place_in):
        return group * GROUP + place_in * 2 + core

    def remote(src, dst, send_sem, recv_sem, target):
        return pltpu.make_async_remote_copy(
            src_ref=src,
            dst_ref=dst,
            send_sem=send_sem,
            recv_sem=recv_sem,
            device_id={"dev": target},
            device_id_type=MESH,
        )

    raw = [
        pltpu.make_async_copy(gate_values, raw_gate, raw_sem.at[0]),
        pltpu.make_async_copy(up_values, raw_up, raw_sem.at[1]),
        pltpu.make_async_copy(down_values, raw_down, raw_sem.at[2]),
    ]
    for copy in raw:
        copy.start()

    barrier = pltpu.get_barrier_semaphore()
    partner = expert * GROUP + chip * 2 + (1 - core)
    pl.semaphore_signal(barrier, inc=1, device_id={"dev": partner}, device_id_type=MESH)

    @pl.loop(1, experts * CHIPS)
    def _(step):
        other = lax.rem(expert * CHIPS + chip + step, experts * CHIPS)
        pl.semaphore_signal(
            barrier, inc=1, device_id={"dev": other * 2 + core}, device_id_type=MESH
        )

    pl.semaphore_wait(barrier, experts * CHIPS)

    def dispatch(step, q):
        group = expert ^ step
        return remote(
            sent.at[step, q],
            got.at[expert, chip],
            sent_sem.at[step, q],
            got_sem.at[expert, chip],
            device(group, q),
        )

    def is_self(step, q):
        return jnp.logical_and(step == 0, q == chip)

    @pl.loop(0, experts)
    def _(turn):
        step = turn ^ (experts - 1)
        for q in range(CHIPS):
            low = tokens[:, 2 * q * width : (2 * q + 1) * width]
            high = tokens[:, (2 * q + 1) * width : (2 * q + 2) * width]
            rows = jnp.dot(
                place[expert ^ step],
                jnp.concatenate([low, high], axis=0),
                preferred_element_type=jnp.float32,
            ).astype(jnp.bfloat16)

            @pl.when(is_self(step, q))
            def _():
                got[expert, chip] = rows

            @pl.when(jnp.logical_not(is_self(step, q)))
            def _():
                sent[step, q] = rows

        for d in (3, 1, 2, 0):

            @pl.when(jnp.logical_not(is_self(step, chip ^ d)))
            def _():
                dispatch(step, chip ^ d).start()

    for copy in raw:
        copy.wait()

    @pl.loop(0, width // BLOCK)
    def _(r):
        span = pl.ds(pl.multiple_of(r * BLOCK, BLOCK), BLOCK)
        gate = (raw_gate[span, :].astype(jnp.float32) * gate_scales[pl.ds(r, 1), :]).astype(
            jnp.bfloat16
        )
        up = (raw_up[span, :].astype(jnp.float32) * up_scales[pl.ds(r, 1), :]).astype(jnp.bfloat16)
        for q in range(CHIPS):
            both[core, q, span, 0:half] = gate[:, q * half : (q + 1) * half]
            both[core, q, span, half:cols] = up[:, q * half : (q + 1) * half]

    wide = [
        remote(both.at[core], both.at[core], wide_sem.at[0], wide_sem.at[1], partner),
        remote(down.at[core], down.at[core], wide_sem.at[2], wide_sem.at[3], partner),
    ]
    wide[0].start()

    @pl.loop(0, raw_down.shape[0] // BLOCK)
    def _(r):
        span = pl.ds(pl.multiple_of(r * BLOCK, BLOCK), BLOCK)
        down[core, span, :] = (
            raw_down[span, :].astype(jnp.float32) * down_scales[pl.ds(r, 1), :]
        ).astype(jnp.bfloat16)

    wide[1].start()
    for copy in wide:
        copy.wait_recv()

    def part_copy(step, d):
        return remote(
            part_out.at[step, d - 1],
            part_in.at[step, d - 1],
            part_out_sem.at[step, d - 1],
            part_in_sem.at[step, d - 1],
            device(expert, chip ^ d),
        )

    def hidden_copy(step, d):
        return remote(
            hidden.at[step, chip],
            hidden.at[step, chip],
            hid_out_sem.at[step, d - 1],
            hid_in_sem.at[step, d - 1],
            device(expert, chip ^ d),
        )

    def back_copy(step, q):
        return remote(
            back_out.at[step, q],
            back_in.at[chip, expert],
            back_out_sem.at[step, q],
            back_in_sem.at[chip, expert],
            device(expert ^ step, q),
        )

    def widen(step):
        source = expert ^ step
        for q in range(CHIPS):

            @pl.when(jnp.logical_not(is_self(step, q)))
            def _():
                remote(
                    sent.at[step, q],
                    got.at[source, q],
                    sent_sem.at[step, q],
                    got_sem.at[source, q],
                    device(source, q),
                ).wait_recv()

        rows = got[source].astype(jnp.float32)
        low = rows[:, :padded].reshape(CHIPS * padded, width).astype(jnp.bfloat16)
        high = rows[:, padded:].reshape(CHIPS * padded, width).astype(jnp.bfloat16)
        for d in (3, 1, 2, 0):
            total = jnp.dot(low, both[0, chip ^ d], preferred_element_type=jnp.float32)
            total = total + jnp.dot(high, both[1, chip ^ d], preferred_element_type=jnp.float32)
            if d == 0:
                own[step] = total
            else:
                part_out[step, d - 1] = total.astype(jnp.bfloat16)
                part_copy(step, d).start()

    def activate(step):
        total = own[step]
        for d in (1, 2, 3):
            part_copy(step, d).wait_recv()
            total = total + part_in[step, d - 1].astype(jnp.float32)
        gate, up = total[:, :half], total[:, half:]
        hidden[step, chip] = (gate / (1.0 + jnp.exp(-gate)) * up).astype(jnp.bfloat16)
        for d in (3, 1, 2):
            hidden_copy(step, d).start()

    def narrow(step):
        for d in (1, 2, 3):
            remote(
                hidden.at[step, chip],
                hidden.at[step, chip ^ d],
                hid_out_sem.at[step, d - 1],
                hid_in_sem.at[step, d - 1],
                device(expert, chip ^ d),
            ).wait_recv()
        whole = jnp.concatenate([hidden[step, q] for q in range(CHIPS)], axis=1)
        low = jnp.dot(whole, down[0], preferred_element_type=jnp.float32)
        high = jnp.dot(whole, down[1], preferred_element_type=jnp.float32)
        for q in range(CHIPS):
            span = slice(q * padded, (q + 1) * padded)
            rows = jnp.concatenate([low[span], high[span]], axis=0).astype(jnp.bfloat16)

            @pl.when(is_self(step, q))
            def _():
                back_in[chip, expert] = rows

            @pl.when(jnp.logical_not(is_self(step, q)))
            def _():
                back_out[step, q] = rows

        for d in (3, 1, 2, 0):

            @pl.when(jnp.logical_not(is_self(step, chip ^ d)))
            def _():
                back_copy(step, chip ^ d).start()

    @pl.loop(0, experts + 1)
    def _(turn):
        @pl.when(turn < experts)
        def _():
            widen(turn ^ (experts - 1))

        @pl.when(turn > 0)
        def _():
            activate((turn - 1) ^ (experts - 1))
            narrow((turn - 1) ^ (experts - 1))

    for q in range(CHIPS):

        @pl.loop(0, experts)
        def _(step):
            @pl.when(jnp.logical_not(is_self(step, q)))
            def _():
                remote(
                    back_out.at[step, q],
                    back_in.at[q, expert ^ step],
                    back_out_sem.at[step, q],
                    back_in_sem.at[q, expert ^ step],
                    device(expert ^ step, q),
                ).wait_recv()

        rows = back_in[q].reshape(experts * 2 * padded, width)
        for h in range(2):
            start = (2 * q + h) * width
            out[:, start : start + width] = jnp.dot(
                weigh[h], rows, preferred_element_type=jnp.float32
            ).astype(jnp.bfloat16)

    for copy in wide:
        copy.wait_send()

    @pl.loop(0, experts)
    def _(step):
        for d in (1, 2, 3):
            part_copy(step, d).wait_send()
            hidden_copy(step, d).wait_send()
        for q in range(CHIPS):

            @pl.when(jnp.logical_not(is_self(step, q)))
            def _():
                dispatch(step, q).wait_send()
                back_copy(step, q).wait_send()


def shards(
    tokens,
    routes,
    route_weight,
    gate_values,
    gate_scales,
    up_values,
    up_scales,
    down_values,
    down_scales,
):
    devices = lax.axis_size("dev")
    experts = devices // GROUP
    tok_count, model = tokens.shape
    top_count = routes.shape[1]
    capacity = min(tok_count, tok_count * top_count * 9 // (8 * experts))
    padded = -(-capacity // 8) * 8
    width, units = gate_values.shape
    cols = 2 * units // CHIPS
    place, weigh = slot_tables(routes, route_weight, experts, padded, capacity)
    spread = functools.partial(jnp.repeat, repeats=BLOCK, axis=1)
    vmem = pl.BlockSpec(memory_space=pltpu.VMEM)
    anywhere = pl.BlockSpec(memory_space=pl.ANY)
    bf16 = jnp.bfloat16
    rows = CHIPS * padded
    dma = pltpu.SemaphoreType.DMA
    return pl.pallas_call(
        functools.partial(kernel, experts, padded),
        out_shape=jax.ShapeDtypeStruct((tok_count, model), bf16),
        in_specs=[vmem, vmem, vmem, anywhere, vmem, anywhere, vmem, anywhere, vmem],
        out_specs=vmem,
        scratch_shapes=[
            pltpu.VMEM((width, units), bf16),
            pltpu.VMEM((width, units), bf16),
            pltpu.VMEM((units, width), bf16),
            pltpu.VMEM((2, CHIPS, width, cols), bf16),
            pltpu.VMEM((2, units, width), bf16),
            pltpu.VMEM((experts, CHIPS, 2 * padded, width), bf16),
            pltpu.VMEM((experts, CHIPS, 2 * padded, width), bf16),
            pltpu.VMEM((experts, rows, cols), jnp.float32),
            pltpu.VMEM((experts, CHIPS - 1, rows, cols), bf16),
            pltpu.VMEM((experts, CHIPS - 1, rows, cols), bf16),
            pltpu.VMEM((experts, CHIPS, rows, cols // 2), bf16),
            pltpu.VMEM((experts, CHIPS, 2 * padded, width), bf16),
            pltpu.VMEM((CHIPS, experts, 2 * padded, width), bf16),
            dma((3,)),
            dma((4,)),
            dma((experts, CHIPS)),
            dma((experts, CHIPS)),
            dma((experts, CHIPS - 1)),
            dma((experts, CHIPS - 1)),
            dma((experts, CHIPS - 1)),
            dma((experts, CHIPS - 1)),
            dma((experts, CHIPS)),
            dma((CHIPS, experts)),
        ],
        compiler_params=pltpu.CompilerParams(
            collective_id=0, has_side_effects=True, vmem_limit_bytes=60 * 1024 * 1024
        ),
    )(
        tokens,
        place,
        weigh,
        gate_values,
        spread(gate_scales),
        up_values,
        spread(up_scales),
        down_values,
        spread(down_scales),
    )


def solution(mesh):
    return jax.shard_map(
        shards,
        mesh=mesh,
        in_specs=(
            P(("rep", "dev"), None),
            P(("rep", "dev"), None),
            P(("rep", "dev"), None),
            P("dev", None),
            P("dev", None),
            P("dev", None),
            P("dev", None),
            P(None, "dev"),
            P(None, "dev"),
        ),
        out_specs=P(("rep", "dev"), None),
        check_vma=False,
    )
```
